128 devices in a mesh: terms: 8 (over x, core), sect: 16 (over y, z).
Axes of the slice: x: 4, y: 4, z: 4, core: 2. Of those that a mesh axis runs over, the one named last changes fastest.
Arguments:
- wavefunction: bfloat16 [32, 32, 128, 128], P('sect'), may hold values from -6 to 6
- left_operator: bfloat16 [192, 32, 128, 128], P('terms', 'sect'), may hold values from -0.5 to 0.5
- right_operator: bfloat16 [192, 32, 128, 128], P('terms', 'sect'), may hold values from -0.0390625 to 0.0390625
- allowed: int32 [32, 32], replicated, may hold values from 0 to 1, as said below
- block_units: int32 [32], replicated, may hold values from 1 to 8
Outputs:
- sigma: bfloat16 [32, 32, 128, 128], P('terms', 'sect')
The draws below stay inside these ranges and needn't reach their ends.
Inputs may be any that keep to these rules, and one draw needn't show every extreme that they name: Each sector carries a charge of 0 or 1; allowed[l, m] is 1 exactly where the charges of l and m add to one common parity, so every row and every column holds at least one 1.
All inputs are finite; a program needn't handle non-finite values.
Results may differ from the reference program's by a relative error of at most 0.0049.
Values may be sent and summed in bfloat16 or wider, within the bound.
No kernel may reach another device: no remote copies, remote signals or barrier semaphores. Data moves between devices by JAX's collectives and lax.ppermute only.
A program may use at most 128 MiB of HBM per device.

```python
import jax
import jax.numpy as jnp
from jax import lax

B = 128
NS = 32
K = 192


def draw_allowed(key, part):
    key = jax.random.fold_in(key, 11)
    key_charge, key_target = jax.random.split(key)
    charges = jax.random.randint(key_charge, (NS,), 0, 2, dtype=jnp.int32)
    charges = charges.at[0].set(0).at[1].set(1)
    target = jax.random.randint(key_target, (), 0, 2, dtype=jnp.int32)
    summed = (charges[:, None] + charges[None, :]) % 2
    return (summed == target).astype(jnp.int32)


def draw_block_units(key, part):
    key = jax.random.fold_in(key, 12)
    key_units, key_order = jax.random.split(key)
    units = jax.random.randint(key_units, (NS,), 6, 9, dtype=jnp.int32)
    order = jax.random.permutation(key_order, NS)
    units = units.at[order[0]].set(1).at[order[1]].set(8)
    return units.astype(jnp.int32)


def level_of(key, extent, cuts, smallest, largest):
    loudness = 1.0
    for axis_at, parts in cuts:
        draws = jax.random.uniform(jax.random.fold_in(jax.random.fold_in(key, 6), axis_at), (parts,), jnp.float32, smallest / len(cuts), largest / len(cuts))
        loudness = loudness * jnp.repeat(jnp.exp(draws), extent[axis_at] // parts).reshape((-1,) + (1,) * (len(extent) - 1 - axis_at))
    return loudness


def bell_draw(stream_key, shape, scale, limit, cuts=(), kind=jnp.bfloat16):
    array = jax.random.normal(stream_key, shape, jnp.float32) * scale
    if len(cuts) > 0:
        array = level_of(stream_key, shape, cuts, -0.22, 0.18) * array
    return jnp.clip(array, min=-limit, max=limit).astype(kind)


def setup_inputs(seed: int = 0) -> dict:
    seeds = jax.random.split(jax.random.key(seed), 6)
    wavefunction = bell_draw(seeds[0], (NS, NS, B, B), 1.0, 6.0, ((0, 16),))
    left_operator = bell_draw(seeds[1], (K, NS, B, B), B ** -0.5, 0.5, ((0, 8), (1, 16)))
    right_operator = bell_draw(seeds[2], (K, NS, B, B), (B * K) ** -0.5, 0.0390625, ((0, 8), (1, 16)))
    allowed = draw_allowed(jax.random.fold_in(seeds[5], 71), 0)
    block_units = draw_block_units(jax.random.fold_in(seeds[5], 71), 0)
    return {"wavefunction": wavefunction, "left_operator": left_operator, "right_operator": right_operator, "allowed": allowed, "block_units": block_units}


def valid_rows(unit_counts, block_width):
    positions = jnp.arange(block_width, dtype=jnp.int32)
    limits = unit_counts * (block_width // 8)
    return (positions[None, :] < limits[:, None]).astype(jnp.bfloat16)


def reference(wavefunction, left_operator, right_operator, allowed, block_units):
    block_width = wavefunction.shape[2]
    row_valid = valid_rows(block_units, block_width)
    weights = allowed.astype(jnp.bfloat16)[:, :, None, None] * row_valid[:, None, :, None] * row_valid[None, :, None, :]
    masked = wavefunction * weights
    masked_wide = masked.astype(jnp.float32)

    def add_term(carry, operators):
        left_one, right_one = operators
        contracted = jnp.einsum("lab,lmbc->lmac", left_one.astype(jnp.float32), masked_wide).astype(jnp.bfloat16)
        carry = carry + jnp.einsum("lmac,mdc->lmad", contracted.astype(jnp.float32), right_one.astype(jnp.float32))
        return carry, None

    start_sum = jnp.zeros(wavefunction.shape, jnp.float32)
    summed, unused = lax.scan(add_term, start_sum, (left_operator, right_operator))
    return (summed * weights.astype(jnp.float32)).astype(jnp.bfloat16)
```

```python
import functools

import jax
import jax.numpy as jnp
from jax import lax
from jax.experimental import pallas as pl
from jax.experimental.pallas import tpu as pltpu
from jax.sharding import Mesh
from jax.sharding import PartitionSpec as P

B = 128
UNIT = B // 8


def shifted(size, step):
    return [(i, (i + step) % size) for i in range(size)]


def products_kernel(
    terms, half, pos, allowed, units, l0, l1, l3, l2a, l2b, r0, r1, r3, r2a, r2b, w, keep, send,
    ls, rs, t, lists, counts, sems,
):
    y, z, x, c = pos[0], pos[1], pos[2], pos[3]
    copies = []

    def fetch(src, dst):
        copy = pltpu.make_async_copy(src, dst, sems.at[len(copies)])
        copy.start()
        copies.append(copy)

    for i in range(2):
        for store, pieces in ((ls, (l0, l1, l2a, l2b, l3)), (rs, (r0, r1, r2a, r2b, r3))):
            p0, p1, p2a, p2b, p3 = pieces
            fetch(p0.at[:, i], store.at[0 + i])
            fetch(p1.at[:, i], store.at[2 + i])
            fetch(p3.at[:, i], store.at[6 + i])
            fetch(p2a.at[:, i], store.at[4 + i, pl.ds(0, half)])
            fetch(p2b.at[:, i], store.at[4 + i, pl.ds(half, terms - half)])

    def left_sector(slot):
        return 8 * lax.rem(y + 4 - slot // 2, 4) + 2 * z + lax.rem(slot, 2)

    def right_local(slot):
        return 2 * lax.rem(z + 4 - slot // 2, 4) + lax.rem(slot, 2)

    for cls in range(2):
        counts[cls] = 0
        counts[2 + cls] = 0

    @pl.loop(0, 8)
    def _(slot):
        cls = allowed[left_sector(slot), 0]
        n = counts[cls]
        lists[8 * cls + n] = slot
        counts[cls] = n + 1
        cls = (allowed[0, 8 * y + right_local(slot)] == allowed[0, 0]).astype(jnp.int32)
        n = counts[2 + cls]
        lists[16 + 8 * cls + n] = slot
        counts[2 + cls] = n + 1

    for copy in copies:
        copy.wait()

    row = lax.broadcasted_iota(jnp.int32, (B, B), 0)
    col = lax.broadcasted_iota(jnp.int32, (B, B), 1)

    def item(lefts, rights):
        nm = len(rights)
        locals_ = [right_local(m) for m in rights]
        for a, l in enumerate(lefts):
            rows = units[left_sector(l)] * UNIT
            blocks = []
            for q in locals_:
                inside = (row < rows) & (col < units[8 * y + q] * UNIT)
                block = w[q, l].astype(jnp.float32)
                blocks.append(jnp.where(inside, block, 0.0).astype(jnp.bfloat16))
            wide = blocks[0] if nm == 1 else jnp.concatenate(blocks, axis=1)
            part = jnp.dot(
                ls[l].reshape(terms * B, B), wide, preferred_element_type=jnp.float32
            ).astype(jnp.bfloat16).reshape(terms, B, nm * B)
            for k in range(terms):
                for b in range(nm):
                    t[b, a * B : (a + 1) * B, k * B : (k + 1) * B] = part[k][:, b * B : (b + 1) * B]
        for b, m in enumerate(rights):
            right = rs[m]
            wide = jnp.concatenate([right[k] for k in range(terms)], axis=1)
            total = lax.dot_general(
                t[b, : len(lefts) * B], wide, (((1,), (1,)), ((), ())),
                preferred_element_type=jnp.float32,
            ).astype(jnp.bfloat16)
            zq = locals_[b] // 2
            e, j = lax.rem(zq, 2), lax.rem(locals_[b], 2)
            mine = zq // 2 == c
            for a, l in enumerate(lefts):
                to = lax.rem(y + 4 - l // 2 + 4 - x, 4)
                i = lax.rem(l, 2)
                block = total[a * B : (a + 1) * B]

                @pl.when(mine)
                def _():
                    keep[to, e, i, j] = block

                @pl.when(jnp.logical_not(mine))
                def _():
                    send[to, e, i, j] = block

    @pl.loop(0, 2)
    def _(cls):
        nl, nm = counts[cls], counts[2 + cls]
        lb, mb = 8 * cls, 16 + 8 * cls

        @pl.loop(0, nl // 2)
        def _(a):
            pair = [lists[lb + 2 * a], lists[lb + 2 * a + 1]]

            @pl.loop(0, nm // 2)
            def _(b):
                item(pair, [lists[mb + 2 * b], lists[mb + 2 * b + 1]])

            @pl.when(lax.rem(nm, 2) == 1)
            def _():
                item(pair, [lists[mb + nm - 1]])

        @pl.when(lax.rem(nl, 2) == 1)
        def _():
            one = [lists[lb + nl - 1]]

            @pl.loop(0, nm // 2)
            def _(b):
                item(one, [lists[mb + 2 * b], lists[mb + 2 * b + 1]])

            @pl.when(lax.rem(nm, 2) == 1)
            def _():
                item(one, [lists[mb + nm - 1]])


def products(pos, allowed, units, lefts, rights, w):
    terms = lefts[0].shape[0]
    half = lefts[3].shape[0]
    smem = pl.BlockSpec(memory_space=pltpu.SMEM)
    anywhere = pl.BlockSpec(memory_space=pl.ANY)
    vmem = pl.BlockSpec(memory_space=pltpu.VMEM)
    out = jax.ShapeDtypeStruct((4, 2, 2, 2, B, B), jnp.bfloat16)
    return pl.pallas_call(
        functools.partial(products_kernel, terms, half),
        out_shape=(out, out),
        in_specs=[smem] * 3 + [anywhere] * 10 + [vmem],
        out_specs=(vmem, vmem),
        scratch_shapes=[
            pltpu.VMEM((8, terms, B, B), jnp.bfloat16),
            pltpu.VMEM((8, terms, B, B), jnp.bfloat16),
            pltpu.VMEM((2, 2 * B, terms * B), jnp.bfloat16),
            pltpu.SMEM((32,), jnp.int32),
            pltpu.SMEM((4,), jnp.int32),
            pltpu.SemaphoreType.DMA((20,)),
        ],
        compiler_params=pltpu.CompilerParams(vmem_limit_bytes=36 * 2**20),
        cost_estimate=pl.CostEstimate(
            flops=64 * terms * 4 * B**3, bytes_accessed=16 * 2**20, transcendentals=0
        ),
    )(pos, allowed, units, *lefts, *rights, w)


def ring(own, axis):
    half = own.shape[0] // 2
    prev = lax.ppermute(own, axis, shifted(4, 1))
    nxt = lax.ppermute(own, axis, shifted(4, -1))
    far_a = lax.ppermute(prev[:half], axis, shifted(4, 1))
    far_b = lax.ppermute(nxt[half:], axis, shifted(4, -1))
    return prev, nxt, far_a, far_b


def shards(wavefunction, left_operator, right_operator, allowed, block_units):
    x, c = lax.axis_index("x"), lax.axis_index("core")
    y, z = lax.axis_index("y"), lax.axis_index("z")
    q = 2 * x + c
    moved = []
    for d in range(4):
        piece = lax.dynamic_slice_in_dim(wavefunction, 8 * ((y + d) % 4) + q, 1, 1)[:, 0]
        moved.append(lax.ppermute(piece, "y", shifted(4, d)) if d else piece)
    w = lax.all_gather(jnp.concatenate(moved, axis=0), ("x", "core"), axis=0, tiled=False)
    lefts = (left_operator, *ring(left_operator, "y"))
    rights = (right_operator, *ring(right_operator, "z"))
    pos = jnp.stack([y, z, x, c]).astype(jnp.int32)
    keep, send = products(pos, allowed, block_units, lefts, rights, w)
    other = lax.ppermute(send, "core", shifted(2, 1))
    total = keep[0].astype(jnp.float32) + other[0].astype(jnp.float32)
    for d in range(1, 4):
        chip = (keep[d].astype(jnp.float32) + other[d].astype(jnp.float32)).astype(jnp.bfloat16)
        total = total + lax.ppermute(chip, "x", shifted(4, d)).astype(jnp.float32)
    lsec = 8 * x + 2 * z + jnp.arange(2)
    msec = (8 * y + 4 * c + jnp.arange(4)).reshape(2, 2)
    inside = jnp.arange(B)[None, :] < block_units[:, None] * UNIT
    mask = (
        (allowed[lsec[None, :, None], msec[:, None, :]] == 1)[..., None, None]
        & inside[lsec][None, :, None, :, None]
        & inside[msec][:, None, :, None, :]
    )
    final = jnp.where(mask, total, 0.0).astype(jnp.bfloat16)
    got = []
    for s in range(2):
        perm = [
            (cc * 4 + zz, (zz // 2) * 4 + 2 * cc + (s ^ (zz & 1)))
            for cc in range(2)
            for zz in range(4)
        ]
        piece = lax.dynamic_index_in_dim(final, s ^ (z & 1), 0, keepdims=False)
        got.append(lax.ppermute(piece, ("core", "z"), perm))
    odd = (z & 1) == 1
    first = jnp.where(odd, got[1], got[0])
    second = jnp.where(odd, got[0], got[1])
    return jnp.concatenate([first, second], axis=0)


def solution(mesh):
    fine = Mesh(mesh.devices.reshape(4, 2, 4, 4), ("x", "core", "y", "z"))
    return jax.shard_map(
        shards,
        mesh=fine,
        in_specs=(
            P(("y", "z"), None, None, None),
            P(("x", "core"), ("y", "z"), None, None),
            P(("x", "core"), ("y", "z"), None, None),
            P(),
            P(),
        ),
        out_specs=P(("x", "core"), ("y", "z"), None, None),
        check_vma=False,
    )
```

```python
import functools

import jax
import jax.numpy as jnp
from jax import lax
from jax.experimental import pallas as pl
from jax.experimental.pallas import tpu as pltpu
from jax.sharding import Mesh
from jax.sharding import PartitionSpec as P

B = 128
UNIT = B // 8
CHUNK = 4


def shifted(size, step):
    return [(i, (i + step) % size) for i in range(size)]


def products_kernel(late, terms, pos, allowed, units, *refs):
    half = terms // 2
    pieces = 5 if late else 3
    lefts, refs = refs[:pieces], refs[pieces:]
    rights, refs = refs[:pieces], refs[pieces:]
    wave, refs = (refs[:1], refs[1:]) if late else (refs[:8], refs[8:])
    if late:
        refs = refs[2:]
    keep, send, *refs = refs
    if not late:
        wave_out, *refs = refs
    ls, rs, w, t, sums, lists, counts, seen, started, sems, out_sems = refs
    y, z, x, c = pos[0], pos[1], pos[2], pos[3]
    whole = []

    def fetch(src, dst, sem):
        copy = pltpu.make_async_copy(src, dst, sem)
        copy.start()
        return copy

    if late:
        new = 2 * lax.rem(z + 2, 4)
        whole.append(
            fetch(wave[0].at[:, pl.ds(6, 2)], w.at[:, pl.ds(6, 2)], sems.at[16])
        )
        whole.append(
            fetch(
                wave[0].at[pl.ds(new, 2), pl.ds(0, 6)],
                w.at[pl.ds(new, 2), pl.ds(0, 6)],
                sems.at[17],
            )
        )
    else:
        for at in range(8):
            chip = lax.rem(x + 4 - at % 4, 4)
            whole.append(fetch(wave[at], w.at[2 * chip + (c ^ (at // 4))], sems.at[16 + at]))
    order = (6, 7, 0, 1, 2, 3, 4, 5) if late else range(6)
    for slot in order:
        for side, (store, parts) in enumerate(((ls, lefts), (rs, rights))):
            sem = sems.at[8 * side + slot]
            i = slot % 2
            if slot < 6:
                fetch(parts[slot // 2].at[:, i], store.at[slot], sem)
            else:
                for part in range(2):
                    fetch(
                        parts[3 + part].at[:, i], store.at[slot, pl.ds(half * part, half)], sem
                    )
    for at in range(16):
        seen[at] = 0

    def ready(side, store, slot):
        at = 8 * side + slot

        @pl.when(seen[at] == 0)
        def _():
            pltpu.make_async_copy(store.at[slot], store.at[slot], sems.at[at]).wait()
            seen[at] = 1

    def shift_of(slot):
        pair = slot // 2
        return jnp.where(pair == 0, 0, jnp.where(pair == 1, 3, pair - 1))

    def left_sector(slot):
        return 8 * lax.rem(y + shift_of(slot), 4) + 2 * z + lax.rem(slot, 2)

    def right_local(slot):
        return 2 * lax.rem(z + shift_of(slot), 4) + lax.rem(slot, 2)

    for at in range(8):
        counts[at] = 0

    def enlist(slot):
        cls = allowed[left_sector(slot), 0]
        n = counts[cls]
        lists[8 * cls + n] = slot
        counts[cls] = n + 1
        cls = (allowed[0, 8 * y + right_local(slot)] == allowed[0, 0]).astype(jnp.int32)
        n = counts[2 + cls]
        lists[16 + 8 * cls + n] = slot
        counts[2 + cls] = n + 1

    if late:
        pl.loop(6, 8)(enlist)
        for at in range(4):
            counts[4 + at] = counts[at]
    pl.loop(0, 6)(enlist)
    if not late:
        for at in range(4):
            counts[4 + at] = counts[at]

    for copy in whole:
        copy.wait()

    if not late:
        row = lax.broadcasted_iota(jnp.int32, (B, B), 0)
        col = lax.broadcasted_iota(jnp.int32, (B, B), 1)

        @pl.loop(0, 8)
        def _(q):
            columns = (col < units[8 * y + q] * UNIT).astype(jnp.float32)
            for l in range(8):
                rows = (row < units[left_sector(l)] * UNIT).astype(jnp.float32)
                w[q, l] = w[q, l] * (rows * columns).astype(jnp.bfloat16)

        passed = fetch(w, wave_out, sems.at[16])
    else:
        counts[8] = 0

    def out_copy(other, to, e, i, j):
        return [
            pltpu.make_async_copy(
                sums.at[other, to, e, i, j],
                out.at[to, e, i, j],
                out_sems.at[(((other * 4 + to) * 2 + e) * 2 + i) * 2 + j],
            )
            for out in (keep, send)
        ]

    def item(left_slots, right_slots):
        nl, nm = len(left_slots), len(right_slots)
        locals_ = [right_local(m) for m in right_slots]
        for l in left_slots:
            ready(0, ls, l)
        for m in right_slots:
            ready(1, rs, m)
        for a, l in enumerate(left_slots):
            blocks = [w[q, l] for q in locals_]
            wide = blocks[0] if nm == 1 else jnp.concatenate(blocks, axis=1)
            for k0 in range(0, terms, CHUNK):
                n = min(CHUNK, terms - k0)
                part = jnp.dot(
                    ls[l, k0 : k0 + n].reshape(n * B, B), wide, preferred_element_type=jnp.float32
                ).astype(jnp.bfloat16).reshape(n, B, nm * B)
                for k in range(n):
                    for b in range(nm):
                        t[b, a * B : (a + 1) * B, (k0 + k) * B : (k0 + k + 1) * B] = part[k][
                            :, b * B : (b + 1) * B
                        ]
        for b, m in enumerate(right_slots):
            right = rs[m]
            wide = jnp.concatenate([right[k] for k in range(terms)], axis=1)
            total = lax.dot_general(
                t[b, : nl * B], wide, (((1,), (1,)), ((), ())), preferred_element_type=jnp.float32
            ).astype(jnp.bfloat16)
            owner = locals_[b] // 2
            e, j = lax.rem(owner, 2), lax.rem(locals_[b], 2)
            other = (owner // 2) ^ c
            for a, l in enumerate(left_slots):
                to = lax.rem(y + shift_of(l) + 4 - x, 4)
                sums[other, to, e, lax.rem(l, 2), j] = total[a * B : (a + 1) * B]
            if late:
                for l in left_slots:
                    to = lax.rem(y + shift_of(l) + 4 - x, 4)
                    kept, sent = out_copy(other, to, e, lax.rem(l, 2), j)
                    pl.when(other == 0)(kept.start)
                    pl.when(other == 1)(sent.start)
                    n = counts[8]
                    started[n] = (((other * 4 + to) * 2 + e) * 2 + lax.rem(l, 2)) * 2 + j
                    counts[8] = n + 1

    def rectangle(cls, l0, nl, m0, nm):
        lb, mb = 8 * cls + l0, 16 + 8 * cls + m0

        @pl.loop(0, nl // 2)
        def _(a):
            pair = [lists[lb + 2 * a], lists[lb + 2 * a + 1]]

            @pl.loop(0, nm // 2)
            def _(b):
                item(pair, [lists[mb + 2 * b], lists[mb + 2 * b + 1]])

            @pl.when(lax.rem(nm, 2) == 1)
            def _():
                item(pair, [lists[mb + nm - 1]])

        @pl.when(lax.rem(nl, 2) == 1)
        def _():
            one = [lists[lb + nl - 1]]

            @pl.loop(0, nm // 2)
            def _(b):
                item(one, [lists[mb + 2 * b], lists[mb + 2 * b + 1]])

            @pl.when(lax.rem(nm, 2) == 1)
            def _():
                item(one, [lists[mb + nm - 1]])

    @pl.loop(0, 4 if late else 2)
    def _(turn):
        cls = lax.rem(turn, 2)
        old = turn // 2
        new_l, all_l = counts[4 + cls], counts[cls]
        new_m, all_m = counts[6 + cls], counts[2 + cls]
        rectangle(
            cls,
            jnp.where(old == 1, new_l, 0),
            jnp.where(old == 1, all_l - new_l, new_l),
            0,
            jnp.where(old == 1, new_m, all_m),
        )

    for slot in order:
        ready(0, ls, slot)
        ready(1, rs, slot)
    if late:

        @pl.loop(0, counts[8])
        def _(n):
            pltpu.make_async_copy(
                sums.at[0, 0, 0, 0, 0], keep.at[0, 0, 0, 0], out_sems.at[started[n]]
            ).wait()
    else:
        done = [fetch(sums.at[0], keep, sems.at[24]), fetch(sums.at[1], send, sems.at[25])]
        for copy in (*done, passed):
            copy.wait()


def products(pos, allowed, units, lefts, rights, wave, before=()):
    terms = lefts[0].shape[0]
    smem = pl.BlockSpec(memory_space=pltpu.SMEM)
    hbm = pl.BlockSpec(memory_space=pl.ANY)
    out = jax.ShapeDtypeStruct((4, 2, 2, 2, B, B), jnp.bfloat16)
    masked = jax.ShapeDtypeStruct((8, 8, B, B), jnp.bfloat16)
    late = bool(before)
    n_in = 3 + 2 * len(lefts) + len(wave)
    return pl.pallas_call(
        functools.partial(products_kernel, late, terms),
        out_shape=(out, out) if late else (out, out, masked),
        in_specs=[smem] * 3 + [hbm] * (n_in - 3 + len(before)),
        out_specs=(hbm,) * (2 if late else 3),
        input_output_aliases={n_in: 0, n_in + 1: 1} if late else {},
        scratch_shapes=[
            pltpu.VMEM((8, terms, B, B), jnp.bfloat16),
            pltpu.VMEM((8, terms, B, B), jnp.bfloat16),
            pltpu.VMEM((8, 8, B, B), jnp.bfloat16),
            pltpu.VMEM((2, 2 * B, terms * B), jnp.bfloat16),
            pltpu.VMEM((2, 4, 2, 2, 2, B, B), jnp.bfloat16),
            pltpu.SMEM((32,), jnp.int32),
            pltpu.SMEM((9,), jnp.int32),
            pltpu.SMEM((16,), jnp.int32),
            pltpu.SMEM((64,), jnp.int32),
            pltpu.SemaphoreType.DMA((26,)),
            pltpu.SemaphoreType.DMA((64,)),
        ],
        compiler_params=pltpu.CompilerParams(vmem_limit_bytes=58 * 2**20),
        cost_estimate=pl.CostEstimate(
            flops=32 * terms * 4 * B**3, bytes_accessed=14 * 2**20, transcendentals=0
        ),
    )(pos, allowed, units, *lefts, *rights, *wave, *before)


def ring_near(own, axis):
    return lax.ppermute(own, axis, shifted(4, 1)), lax.ppermute(own, axis, shifted(4, -1))


def far_half(near):
    half = near[0].shape[0] // 2
    return near[0][:half], near[1][half:]


def ring_far(halves, axis):
    return (
        lax.ppermute(halves[0], axis, shifted(4, 1)),
        lax.ppermute(halves[1], axis, shifted(4, -1)),
    )


def swapped(size, bit):
    return [(i, i ^ bit) for i in range(size)]


def gather_wave(wavefunction, y, q, operators):
    def toward(owner):
        return lax.dynamic_slice_in_dim(wavefunction, 8 * owner + q, 1, 1)[:, 0]

    moved = [lax.ppermute(toward((y + d) % 4), "y", shifted(4, d)) for d in (1, 3, 2)]
    left, right = operators
    first, right = lax.optimization_barrier((moved[0], right))
    moved, left = lax.optimization_barrier(([first] + moved[1:], left))
    operators = left, right
    mine = jnp.concatenate([toward(y)] + moved)
    row = [mine] + [lax.ppermute(mine, "x", shifted(4, d)) for d in (1, 2, 3)]
    return row, operators


def share_wave(row):
    return (*row, *(lax.ppermute(part, "core", swapped(2, 1)) for part in row))


def add_cores(keep, send):
    other = lax.ppermute(send, "core", shifted(2, 1))
    both = [keep[d].astype(jnp.float32) + other[d].astype(jnp.float32) for d in range(4)]
    return both[0], [part.astype(jnp.bfloat16) for part in both[1:]]


def add_send(chips):
    return [lax.ppermute(part, "x", shifted(4, d + 1)) for d, part in enumerate(chips)]


def add_chips(own, chips):
    return (own + sum(part.astype(jnp.float32) for part in chips)).astype(jnp.bfloat16)


def shards(wavefunction, left_operator, right_operator, allowed, block_units):
    x, c = lax.axis_index("x"), lax.axis_index("core")
    y, z = lax.axis_index("y"), lax.axis_index("z")
    q = 2 * x + c
    row, (left_operator, right_operator) = gather_wave(
        wavefunction, y, q, (left_operator, right_operator)
    )
    near_l, near_r = ring_near(left_operator, "y"), ring_near(right_operator, "z")
    row, *near_l = lax.optimization_barrier((row, *near_l))
    wave = share_wave(row)
    lefts, rights = (left_operator, *near_l), (right_operator, *near_r)
    pos = jnp.stack([y, z, x, c]).astype(jnp.int32)
    far_l, far_r = far_half(near_l), far_half(near_r)
    *sums, masked = products(pos, allowed, block_units, lefts, rights, wave)
    lefts = (*lefts, *ring_far(far_l, "y"))
    rights = (*rights, *ring_far(far_r, "z"))
    keep, send = products(pos, allowed, block_units, lefts, rights, (masked,), sums)
    own, chips = add_cores(keep, send)
    final = add_chips(own, add_send(chips))

    got = []
    for s in range(2):
        perm = [
            (cc * 4 + zz, (zz // 2) * 4 + 2 * cc + (s ^ (zz & 1)))
            for cc in range(2)
            for zz in range(4)
        ]
        piece = lax.dynamic_index_in_dim(final, s ^ (z & 1), 0, keepdims=False)
        got.append(lax.ppermute(piece, ("core", "z"), perm))
    odd = (z & 1) == 1
    first = jnp.where(odd, got[1], got[0])
    second = jnp.where(odd, got[0], got[1])
    out = jnp.concatenate([first, second], axis=0)
    l0, m0 = 8 * x + 4 * c, 8 * y + 2 * z
    pairs = lax.dynamic_slice(allowed, (l0, m0), (4, 2))
    inside = jnp.arange(B)[None, :] < block_units[:, None] * UNIT
    mask = (
        (pairs == 1)[:, :, None, None]
        & lax.dynamic_slice_in_dim(inside, l0, 4, 0)[:, None, :, None]
        & lax.dynamic_slice_in_dim(inside, m0, 2, 0)[None, :, None, :]
    )
    return jnp.where(mask, out, jnp.bfloat16(0))


def solution(mesh):
    fine = Mesh(mesh.devices.reshape(4, 2, 4, 4), ("x", "core", "y", "z"))
    return jax.shard_map(
        shards,
        mesh=fine,
        in_specs=(
            P(("y", "z"), None, None, None),
            P(("x", "core"), ("y", "z"), None, None),
            P(("x", "core"), ("y", "z"), None, None),
            P(),
            P(),
        ),
        out_specs=P(("x", "core"), ("y", "z"), None, None),
        check_vma=False,
    )
```

```python
import functools

import jax
import jax.numpy as jnp
from jax import lax
from jax.experimental import pallas as pl
from jax.experimental.pallas import tpu as pltpu
from jax.sharding import Mesh
from jax.sharding import PartitionSpec as P

B = 128
UNIT = B // 8
CHUNK = 4


def shifted(size, step):
    return [(i, (i + step) % size) for i in range(size)]


def products_kernel(late, terms, pos, allowed, units, *refs):
    half = terms // 2
    pieces = 5 if late else 3
    lefts, refs = refs[:pieces], refs[pieces:]
    rights, refs = refs[:pieces], refs[pieces:]
    wave, refs = (refs[:1], refs[1:]) if late else (refs[:8], refs[8:])
    if late:
        refs = refs[2:]
    keep, send, *refs = refs
    if not late:
        wave_out, *refs = refs
    ls, rs, w, t, sums, lists, counts, seen, started, sems, out_sems = refs
    y, z, x, c = pos[0], pos[1], pos[2], pos[3]
    whole = []

    def fetch(src, dst, sem):
        copy = pltpu.make_async_copy(src, dst, sem)
        copy.start()
        return copy

    if late:
        new = 2 * lax.rem(z + 2, 4)
        whole.append(
            fetch(wave[0].at[:, pl.ds(6, 2)], w.at[:, pl.ds(6, 2)], sems.at[16])
        )
        whole.append(
            fetch(
                wave[0].at[pl.ds(new, 2), pl.ds(0, 6)],
                w.at[pl.ds(new, 2), pl.ds(0, 6)],
                sems.at[17],
            )
        )
    else:
        for at in range(8):
            chip = lax.rem(x + 4 - at % 4, 4)
            whole.append(fetch(wave[at], w.at[2 * chip + (c ^ (at // 4))], sems.at[16 + at]))
    order = (6, 7, 0, 1, 2, 3, 4, 5) if late else range(6)
    turns = [(side, slot) for slot in order for side in range(2)]
    if late:
        turns.sort(key=lambda turn: (turn[0] == 0 and turn[1] < 6))
    for side, slot in turns:
        store, parts = ((ls, lefts), (rs, rights))[side]
        sem = sems.at[8 * side + slot]
        i = slot % 2
        if slot < 6:
            fetch(parts[slot // 2].at[:, i], store.at[slot], sem)
        else:
            for part in range(2):
                fetch(parts[3 + part].at[:, i], store.at[slot, pl.ds(half * part, half)], sem)
    for at in range(16):
        seen[at] = 0

    def ready(side, store, slot):
        at = 8 * side + slot

        @pl.when(seen[at] == 0)
        def _():
            pltpu.make_async_copy(store.at[slot], store.at[slot], sems.at[at]).wait()
            seen[at] = 1

    def shift_of(slot):
        pair = slot // 2
        return jnp.where(pair == 0, 0, jnp.where(pair == 1, 3, pair - 1))

    def left_sector(slot):
        return 8 * lax.rem(y + shift_of(slot), 4) + 2 * z + lax.rem(slot, 2)

    def right_local(slot):
        return 2 * lax.rem(z + shift_of(slot), 4) + lax.rem(slot, 2)

    for at in range(8):
        counts[at] = 0

    def enlist(slot):
        cls = allowed[left_sector(slot), 0]
        n = counts[cls]
        lists[8 * cls + n] = slot
        counts[cls] = n + 1
        cls = (allowed[0, 8 * y + right_local(slot)] == allowed[0, 0]).astype(jnp.int32)
        n = counts[2 + cls]
        lists[16 + 8 * cls + n] = slot
        counts[2 + cls] = n + 1

    if late:
        pl.loop(6, 8)(enlist)
        for at in range(4):
            counts[4 + at] = counts[at]
    pl.loop(0, 6)(enlist)
    if not late:
        for at in range(4):
            counts[4 + at] = counts[at]

    for copy in whole:
        copy.wait()

    if not late:
        row = lax.broadcasted_iota(jnp.int32, (B, B), 0)
        col = lax.broadcasted_iota(jnp.int32, (B, B), 1)

        @pl.loop(0, 8)
        def _(q):
            columns = (col < units[8 * y + q] * UNIT).astype(jnp.float32)
            for l in range(8):
                rows = (row < units[left_sector(l)] * UNIT).astype(jnp.float32)
                w[q, l] = w[q, l] * (rows * columns).astype(jnp.bfloat16)

        passed = fetch(w, wave_out, sems.at[16])
    counts[8] = 0

    def out_copy(other, to, e, i, j):
        return [
            pltpu.make_async_copy(
                sums.at[other, to, e, i, j],
                out.at[to, e, i, j],
                out_sems.at[(((other * 4 + to) * 2 + e) * 2 + i) * 2 + j],
            )
            for out in (keep, send)
        ]

    def item(left_slots, right_slots):
        nl, nm = len(left_slots), len(right_slots)
        locals_ = [right_local(m) for m in right_slots]
        for l in left_slots:
            ready(0, ls, l)
        for m in right_slots:
            ready(1, rs, m)
        for a, l in enumerate(left_slots):
            blocks = [w[q, l] for q in locals_]
            wide = blocks[0] if nm == 1 else jnp.concatenate(blocks, axis=1)
            for k0 in range(0, terms, CHUNK):
                n = min(CHUNK, terms - k0)
                part = jnp.dot(
                    ls[l, k0 : k0 + n].reshape(n * B, B), wide, preferred_element_type=jnp.float32
                ).astype(jnp.bfloat16).reshape(n, B, nm * B)
                for k in range(n):
                    for b in range(nm):
                        t[b, a * B : (a + 1) * B, (k0 + k) * B : (k0 + k + 1) * B] = part[k][
                            :, b * B : (b + 1) * B
                        ]
        for b, m in enumerate(right_slots):
            right = rs[m]
            wide = jnp.concatenate([right[k] for k in range(terms)], axis=1)
            total = lax.dot_general(
                t[b, : nl * B], wide, (((1,), (1,)), ((), ())), preferred_element_type=jnp.float32
            ).astype(jnp.bfloat16)
            owner = locals_[b] // 2
            e, j = lax.rem(owner, 2) ^ lax.rem(z, 2), lax.rem(locals_[b], 2)
            other = (owner // 2) ^ c
            for a, l in enumerate(left_slots):
                to = lax.rem(y + shift_of(l) + 4 - x, 4)
                sums[other, to, e, lax.rem(l, 2), j] = total[a * B : (a + 1) * B]
            for l in left_slots:
                to = lax.rem(y + shift_of(l) + 4 - x, 4)
                kept, sent = out_copy(other, to, e, lax.rem(l, 2), j)
                pl.when(other == 0)(kept.start)
                pl.when(other == 1)(sent.start)
                n = counts[8]
                started[n] = (((other * 4 + to) * 2 + e) * 2 + lax.rem(l, 2)) * 2 + j
                counts[8] = n + 1

    def rectangle(cls, l0, nl, m0, nm):
        lb, mb = 8 * cls + l0, 16 + 8 * cls + m0

        @pl.loop(0, nl // 2)
        def _(a):
            pair = [lists[lb + 2 * a], lists[lb + 2 * a + 1]]

            @pl.loop(0, nm // 2)
            def _(b):
                item(pair, [lists[mb + 2 * b], lists[mb + 2 * b + 1]])

            @pl.when(lax.rem(nm, 2) == 1)
            def _():
                item(pair, [lists[mb + nm - 1]])

        @pl.when(lax.rem(nl, 2) == 1)
        def _():
            one = [lists[lb + nl - 1]]

            @pl.loop(0, nm // 2)
            def _(b):
                item(one, [lists[mb + 2 * b], lists[mb + 2 * b + 1]])

            @pl.when(lax.rem(nm, 2) == 1)
            def _():
                item(one, [lists[mb + nm - 1]])

    @pl.loop(0, 4 if late else 2)
    def _(turn):
        cls = lax.rem(turn, 2)
        old = turn // 2
        new_l, all_l = counts[4 + cls], counts[cls]
        new_m, all_m = counts[6 + cls], counts[2 + cls]
        rectangle(
            cls,
            jnp.where(old == 1, new_l, 0),
            jnp.where(old == 1, all_l - new_l, new_l),
            0,
            jnp.where(old == 1, new_m, all_m),
        )

    for slot in order:
        ready(0, ls, slot)
        ready(1, rs, slot)

    @pl.loop(0, counts[8])
    def _(n):
        pltpu.make_async_copy(
            sums.at[0, 0, 0, 0, 0], keep.at[0, 0, 0, 0], out_sems.at[started[n]]
        ).wait()

    if not late:
        passed.wait()


def products(pos, allowed, units, lefts, rights, wave, before=()):
    terms = lefts[0].shape[0]
    smem = pl.BlockSpec(memory_space=pltpu.SMEM)
    hbm = pl.BlockSpec(memory_space=pl.ANY)
    out = jax.ShapeDtypeStruct((4, 2, 2, 2, B, B), jnp.bfloat16)
    masked = jax.ShapeDtypeStruct((8, 8, B, B), jnp.bfloat16)
    late = bool(before)
    n_in = 3 + 2 * len(lefts) + len(wave)
    return pl.pallas_call(
        functools.partial(products_kernel, late, terms),
        out_shape=(out, out) if late else (out, out, masked),
        in_specs=[smem] * 3 + [hbm] * (n_in - 3 + len(before)),
        out_specs=(hbm,) * (2 if late else 3),
        input_output_aliases={n_in: 0, n_in + 1: 1} if late else {},
        scratch_shapes=[
            pltpu.VMEM((8, terms, B, B), jnp.bfloat16),
            pltpu.VMEM((8, terms, B, B), jnp.bfloat16),
            pltpu.VMEM((8, 8, B, B), jnp.bfloat16),
            pltpu.VMEM((2, 2 * B, terms * B), jnp.bfloat16),
            pltpu.VMEM((2, 4, 2, 2, 2, B, B), jnp.bfloat16),
            pltpu.SMEM((32,), jnp.int32),
            pltpu.SMEM((9,), jnp.int32),
            pltpu.SMEM((16,), jnp.int32),
            pltpu.SMEM((64,), jnp.int32),
            pltpu.SemaphoreType.DMA((26,)),
            pltpu.SemaphoreType.DMA((64,)),
        ],
        compiler_params=pltpu.CompilerParams(vmem_limit_bytes=58 * 2**20),
        cost_estimate=pl.CostEstimate(
            flops=32 * terms * 4 * B**3, bytes_accessed=14 * 2**20, transcendentals=0
        ),
    )(pos, allowed, units, *lefts, *rights, *wave, *before)


def ring_near(own, axis):
    return lax.ppermute(own, axis, shifted(4, 1)), lax.ppermute(own, axis, shifted(4, -1))


def far_half(near):
    half = near[0].shape[0] // 2
    return near[0][:half], near[1][half:]


def ring_far(halves, axis):
    return (
        lax.ppermute(halves[0], axis, shifted(4, 1)),
        lax.ppermute(halves[1], axis, shifted(4, -1)),
    )


def swapped(size, bit):
    return [(i, i ^ bit) for i in range(size)]


def gather_wave(wavefunction, y, q, operators):
    def toward(owner):
        return lax.dynamic_slice_in_dim(wavefunction, 8 * owner + q, 1, 1)[:, 0]

    moved = [lax.ppermute(toward((y + d) % 4), "y", shifted(4, d)) for d in (1, 3, 2)]
    left, right = operators
    first, right = lax.optimization_barrier((moved[0], right))
    moved, left = lax.optimization_barrier(([first] + moved[1:], left))
    operators = left, right
    mine = jnp.concatenate([toward(y)] + moved)
    row = [mine] + [lax.ppermute(mine, "x", shifted(4, d)) for d in (1, 2, 3)]
    return row, operators


def share_wave(row):
    return (*row, *(lax.ppermute(part, "core", swapped(2, 1)) for part in row))


def add_cores(keep, other, s):
    both = [keep[d, s].astype(jnp.float32) + other[d, s].astype(jnp.float32) for d in range(4)]
    return both[0], [part.astype(jnp.bfloat16) for part in both[1:]]


def add_send(chips):
    return [lax.ppermute(part, "x", shifted(4, d + 1)) for d, part in enumerate(chips)]


def add_chips(own, chips):
    return (own + sum(part.astype(jnp.float32) for part in chips)).astype(jnp.bfloat16)


def shards(wavefunction, left_operator, right_operator, allowed, block_units):
    x, c = lax.axis_index("x"), lax.axis_index("core")
    y, z = lax.axis_index("y"), lax.axis_index("z")
    q = 2 * x + c
    row, (left_operator, right_operator) = gather_wave(
        wavefunction, y, q, (left_operator, right_operator)
    )
    near_l, near_r = ring_near(left_operator, "y"), ring_near(right_operator, "z")
    row, *near_l = lax.optimization_barrier((row, *near_l))
    wave = share_wave(row)
    lefts, rights = (left_operator, *near_l), (right_operator, *near_r)
    pos = jnp.stack([y, z, x, c]).astype(jnp.int32)
    far_l, far_r = far_half(near_l), far_half(near_r)
    *sums, masked = products(pos, allowed, block_units, lefts, rights, wave)
    lefts = (*lefts, *ring_far(far_l, "y"))
    rights = (*rights, *ring_far(far_r, "z"))
    keep, send = products(pos, allowed, block_units, lefts, rights, (masked,), sums)
    other = lax.ppermute(send, "core", shifted(2, 1))
    halves = [add_cores(keep, other, s) for s in range(2)]
    halves = [(own, add_send(chips)) for own, chips in halves]

    got = []
    for s in range(2):
        perm = [
            (cc * 4 + zz, (zz // 2) * 4 + 2 * cc + (s ^ (zz & 1)))
            for cc in range(2)
            for zz in range(4)
        ]
        half, got = lax.optimization_barrier((halves[s], got))
        got.append(lax.ppermute(add_chips(*half), ("core", "z"), perm))
    odd = (z & 1) == 1
    first = jnp.where(odd, got[1], got[0])
    second = jnp.where(odd, got[0], got[1])
    out = jnp.concatenate([first, second], axis=0)
    l0, m0 = 8 * x + 4 * c, 8 * y + 2 * z
    pairs = lax.dynamic_slice(allowed, (l0, m0), (4, 2))
    inside = jnp.arange(B)[None, :] < block_units[:, None] * UNIT
    mask = (
        (pairs == 1)[:, :, None, None]
        & lax.dynamic_slice_in_dim(inside, l0, 4, 0)[:, None, :, None]
        & lax.dynamic_slice_in_dim(inside, m0, 2, 0)[None, :, None, :]
    )
    return jnp.where(mask, out, jnp.bfloat16(0))


def solution(mesh):
    fine = Mesh(mesh.devices.reshape(4, 2, 4, 4), ("x", "core", "y", "z"))
    return jax.shard_map(
        shards,
        mesh=fine,
        in_specs=(
            P(("y", "z"), None, None, None),
            P(("x", "core"), ("y", "z"), None, None),
            P(("x", "core"), ("y", "z"), None, None),
            P(),
            P(),
        ),
        out_specs=P(("x", "core"), ("y", "z"), None, None),
        check_vma=False,
    )
```

```python
import functools

import jax
import jax.numpy as jnp
from jax import lax
from jax.experimental import pallas as pl
from jax.experimental.pallas import tpu as pltpu
from jax.sharding import Mesh
from jax.sharding import PartitionSpec as P

B = 128
UNIT = B // 8
CHUNK = 4


def shifted(size, step):
    return [(i, (i + step) % size) for i in range(size)]


def products_kernel(late, terms, pos, allowed, units, *refs):
    half = terms // 2
    pieces = 5 if late else 3
    lefts, refs = refs[:pieces], refs[pieces:]
    rights, refs = refs[:pieces], refs[pieces:]
    wave, refs = (refs[:1], refs[1:]) if late else (refs[:8], refs[8:])
    if late:
        refs = refs[4:]
    outs, refs = refs[:4], refs[4:]
    if not late:
        wave_out, *refs = refs
    ls, rs, w, t, sums, lists, counts, seen, started, sems, out_sems = refs
    y, z, x, c = pos[0], pos[1], pos[2], pos[3]
    whole = []

    def fetch(src, dst, sem):
        copy = pltpu.make_async_copy(src, dst, sem)
        copy.start()
        return copy

    if late:
        new = 2 * lax.rem(z + 2, 4)
        whole.append(
            fetch(wave[0].at[:, pl.ds(6, 2)], w.at[:, pl.ds(6, 2)], sems.at[16])
        )
        whole.append(
            fetch(
                wave[0].at[pl.ds(new, 2), pl.ds(0, 6)],
                w.at[pl.ds(new, 2), pl.ds(0, 6)],
                sems.at[17],
            )
        )
    else:
        for at in range(8):
            chip = lax.rem(x + 4 - at % 4, 4)
            whole.append(fetch(wave[at], w.at[2 * chip + (c ^ (at // 4))], sems.at[16 + at]))
    order = (6, 7, 0, 1, 2, 3, 4, 5) if late else range(6)
    turns = [(side, slot) for slot in order for side in range(2)]
    if late:
        turns.sort(key=lambda turn: (turn[0] == 0 and turn[1] < 6))
    for side, slot in turns:
        store, parts = ((ls, lefts), (rs, rights))[side]
        sem = sems.at[8 * side + slot]
        i = slot % 2
        if slot < 6:
            fetch(parts[slot // 2].at[:, i], store.at[slot], sem)
        else:
            for part in range(2):
                fetch(parts[3 + part].at[:, i], store.at[slot, pl.ds(half * part, half)], sem)
    for at in range(16):
        seen[at] = 0

    def ready(side, store, slot):
        at = 8 * side + slot

        @pl.when(seen[at] == 0)
        def _():
            pltpu.make_async_copy(store.at[slot], store.at[slot], sems.at[at]).wait()
            seen[at] = 1

    def shift_of(slot):
        pair = slot // 2
        return jnp.where(pair == 0, 0, jnp.where(pair == 1, 3, pair - 1))

    def left_sector(slot):
        return 8 * lax.rem(y + shift_of(slot), 4) + 2 * z + lax.rem(slot, 2)

    def right_local(slot):
        return 2 * lax.rem(z + shift_of(slot), 4) + lax.rem(slot, 2)

    for at in range(8):
        counts[at] = 0

    def enlist(slot):
        cls = allowed[left_sector(slot), 0]
        n = counts[cls]
        lists[8 * cls + n] = slot
        counts[cls] = n + 1
        cls = (allowed[0, 8 * y + right_local(slot)] == allowed[0, 0]).astype(jnp.int32)
        n = counts[2 + cls]
        lists[16 + 8 * cls + n] = slot
        counts[2 + cls] = n + 1

    if late:
        pl.loop(6, 8)(enlist)
        for at in range(4):
            counts[4 + at] = counts[at]
    pl.loop(0, 6)(enlist)
    if not late:
        for at in range(4):
            counts[4 + at] = counts[at]

    for copy in whole:
        copy.wait()

    if not late:
        row = lax.broadcasted_iota(jnp.int32, (B, B), 0)
        col = lax.broadcasted_iota(jnp.int32, (B, B), 1)

        @pl.loop(0, 8)
        def _(q):
            columns = (col < units[8 * y + q] * UNIT).astype(jnp.float32)
            for l in range(8):
                rows = (row < units[left_sector(l)] * UNIT).astype(jnp.float32)
                w[q, l] = w[q, l] * (rows * columns).astype(jnp.bfloat16)

        passed = fetch(w, wave_out, sems.at[16])
    counts[8] = 0

    def out_copy(other, to, e, i, j):
        return [
            pltpu.make_async_copy(
                sums.at[other, to, e, i, j],
                out.at[to, i, j],
                out_sems.at[(((other * 4 + to) * 2 + e) * 2 + i) * 2 + j],
            )
            for out in outs
        ]

    def item(left_slots, right_slots):
        nl, nm = len(left_slots), len(right_slots)
        locals_ = [right_local(m) for m in right_slots]
        for l in left_slots:
            ready(0, ls, l)
        for m in right_slots:
            ready(1, rs, m)
        for a, l in enumerate(left_slots):
            blocks = [w[q, l] for q in locals_]
            wide = blocks[0] if nm == 1 else jnp.concatenate(blocks, axis=1)
            for k0 in range(0, terms, CHUNK):
                n = min(CHUNK, terms - k0)
                part = jnp.dot(
                    ls[l, k0 : k0 + n].reshape(n * B, B), wide, preferred_element_type=jnp.float32
                ).astype(jnp.bfloat16).reshape(n, B, nm * B)
                for k in range(n):
                    for b in range(nm):
                        t[b, a * B : (a + 1) * B, (k0 + k) * B : (k0 + k + 1) * B] = part[k][
                            :, b * B : (b + 1) * B
                        ]
        for b, m in enumerate(right_slots):
            right = rs[m]
            wide = jnp.concatenate([right[k] for k in range(terms)], axis=1)
            total = lax.dot_general(
                t[b, : nl * B], wide, (((1,), (1,)), ((), ())), preferred_element_type=jnp.float32
            ).astype(jnp.bfloat16)
            owner = locals_[b] // 2
            e, j = lax.rem(owner, 2) ^ lax.rem(z, 2), lax.rem(locals_[b], 2)
            other = (owner // 2) ^ c
            for a, l in enumerate(left_slots):
                to = lax.rem(y + shift_of(l) + 4 - x, 4)
                sums[other, to, e, lax.rem(l, 2), j] = total[a * B : (a + 1) * B]
            for l in left_slots:
                to = lax.rem(y + shift_of(l) + 4 - x, 4)
                for at, copy in enumerate(out_copy(other, to, e, lax.rem(l, 2), j)):
                    pl.when(2 * other + e == at)(copy.start)
                n = counts[8]
                started[n] = (((other * 4 + to) * 2 + e) * 2 + lax.rem(l, 2)) * 2 + j
                counts[8] = n + 1

    def rectangle(cls, l0, nl, m0, nm):
        lb, mb = 8 * cls + l0, 16 + 8 * cls + m0

        @pl.loop(0, nl // 2)
        def _(a):
            pair = [lists[lb + 2 * a], lists[lb + 2 * a + 1]]

            @pl.loop(0, nm // 2)
            def _(b):
                item(pair, [lists[mb + 2 * b], lists[mb + 2 * b + 1]])

            @pl.when(lax.rem(nm, 2) == 1)
            def _():
                item(pair, [lists[mb + nm - 1]])

        @pl.when(lax.rem(nl, 2) == 1)
        def _():
            one = [lists[lb + nl - 1]]

            @pl.loop(0, nm // 2)
            def _(b):
                item(one, [lists[mb + 2 * b], lists[mb + 2 * b + 1]])

            @pl.when(lax.rem(nm, 2) == 1)
            def _():
                item(one, [lists[mb + nm - 1]])

    @pl.loop(0, 4 if late else 2)
    def _(turn):
        cls = lax.rem(turn, 2)
        old = turn // 2
        new_l, all_l = counts[4 + cls], counts[cls]
        new_m, all_m = counts[6 + cls], counts[2 + cls]
        rectangle(
            cls,
            jnp.where(old == 1, new_l, 0),
            jnp.where(old == 1, all_l - new_l, new_l),
            0,
            jnp.where(old == 1, new_m, all_m),
        )

    for slot in order:
        ready(0, ls, slot)
        ready(1, rs, slot)

    @pl.loop(0, counts[8])
    def _(n):
        pltpu.make_async_copy(
            sums.at[0, 0, 0, 0, 0], outs[0].at[0, 0, 0], out_sems.at[started[n]]
        ).wait()

    if not late:
        passed.wait()


def products(pos, allowed, units, lefts, rights, wave, before=()):
    terms = lefts[0].shape[0]
    smem = pl.BlockSpec(memory_space=pltpu.SMEM)
    hbm = pl.BlockSpec(memory_space=pl.ANY)
    out = jax.ShapeDtypeStruct((4, 2, 2, B, B), jnp.bfloat16)
    masked = jax.ShapeDtypeStruct((8, 8, B, B), jnp.bfloat16)
    late = bool(before)
    n_in = 3 + 2 * len(lefts) + len(wave)
    return pl.pallas_call(
        functools.partial(products_kernel, late, terms),
        out_shape=(out,) * 4 if late else (out,) * 4 + (masked,),
        in_specs=[smem] * 3 + [hbm] * (n_in - 3 + len(before)),
        out_specs=(hbm,) * (4 if late else 5),
        input_output_aliases={n_in + at: at for at in range(len(before))},
        scratch_shapes=[
            pltpu.VMEM((8, terms, B, B), jnp.bfloat16),
            pltpu.VMEM((8, terms, B, B), jnp.bfloat16),
            pltpu.VMEM((8, 8, B, B), jnp.bfloat16),
            pltpu.VMEM((2, 2 * B, terms * B), jnp.bfloat16),
            pltpu.VMEM((2, 4, 2, 2, 2, B, B), jnp.bfloat16),
            pltpu.SMEM((32,), jnp.int32),
            pltpu.SMEM((9,), jnp.int32),
            pltpu.SMEM((16,), jnp.int32),
            pltpu.SMEM((64,), jnp.int32),
            pltpu.SemaphoreType.DMA((26,)),
            pltpu.SemaphoreType.DMA((64,)),
        ],
        compiler_params=pltpu.CompilerParams(vmem_limit_bytes=58 * 2**20),
        cost_estimate=pl.CostEstimate(
            flops=32 * terms * 4 * B**3, bytes_accessed=14 * 2**20, transcendentals=0
        ),
    )(pos, allowed, units, *lefts, *rights, *wave, *before)


def ring_near(own, axis):
    return lax.ppermute(own, axis, shifted(4, 1)), lax.ppermute(own, axis, shifted(4, -1))


def far_half(near):
    half = near[0].shape[0] // 2
    return near[0][:half], near[1][half:]


def ring_far(halves, axis):
    return (
        lax.ppermute(halves[0], axis, shifted(4, 1)),
        lax.ppermute(halves[1], axis, shifted(4, -1)),
    )


def swapped(size, bit):
    return [(i, i ^ bit) for i in range(size)]


def gather_wave(wavefunction, y, q, operators):
    def toward(owner):
        return lax.dynamic_slice_in_dim(wavefunction, 8 * owner + q, 1, 1)[:, 0]

    moved = [lax.ppermute(toward((y + d) % 4), "y", shifted(4, d)) for d in (1, 3, 2)]
    left, right = operators
    first, right = lax.optimization_barrier((moved[0], right))
    moved, left = lax.optimization_barrier(([first] + moved[1:], left))
    operators = left, right
    mine = jnp.concatenate([toward(y)] + moved)
    row = [mine] + [lax.ppermute(mine, "x", shifted(4, d)) for d in (1, 2, 3)]
    return row, operators


def share_wave(row):
    return (*row, *(lax.ppermute(part, "core", swapped(2, 1)) for part in row))


def add_cores(keep, send):
    other = lax.ppermute(send, "core", shifted(2, 1))
    both = [keep[d].astype(jnp.float32) + other[d].astype(jnp.float32) for d in range(4)]
    return both[0], [part.astype(jnp.bfloat16) for part in both[1:]]


def add_send(chips):
    return [lax.ppermute(part, "x", shifted(4, d + 1)) for d, part in enumerate(chips)]


def add_chips(own, chips):
    return (own + sum(part.astype(jnp.float32) for part in chips)).astype(jnp.bfloat16)


def shards(wavefunction, left_operator, right_operator, allowed, block_units):
    x, c = lax.axis_index("x"), lax.axis_index("core")
    y, z = lax.axis_index("y"), lax.axis_index("z")
    q = 2 * x + c
    row, (left_operator, right_operator) = gather_wave(
        wavefunction, y, q, (left_operator, right_operator)
    )
    near_l, near_r = ring_near(left_operator, "y"), ring_near(right_operator, "z")
    row, *near_l = lax.optimization_barrier((row, *near_l))
    wave = share_wave(row)
    lefts, rights = (left_operator, *near_l), (right_operator, *near_r)
    pos = jnp.stack([y, z, x, c]).astype(jnp.int32)
    far_l, far_r = far_half(near_l), far_half(near_r)
    *sums, masked = products(pos, allowed, block_units, lefts, rights, wave)
    lefts = (*lefts, *ring_far(far_l, "y"))
    rights = (*rights, *ring_far(far_r, "z"))
    sums = products(pos, allowed, block_units, lefts, rights, (masked,), sums)
    halves = [add_cores(sums[s], sums[2 + s]) for s in range(2)]
    halves = [(own, add_send(chips)) for own, chips in halves]

    got = []
    for s in range(2):
        perm = [
            (cc * 4 + zz, (zz // 2) * 4 + 2 * cc + (s ^ (zz & 1)))
            for cc in range(2)
            for zz in range(4)
        ]
        half, got = lax.optimization_barrier((halves[s], got))
        got.append(lax.ppermute(add_chips(*half), ("core", "z"), perm))
    odd = (z & 1) == 1
    first = jnp.where(odd, got[1], got[0])
    second = jnp.where(odd, got[0], got[1])
    out = jnp.concatenate([first, second], axis=0)
    l0, m0 = 8 * x + 4 * c, 8 * y + 2 * z
    pairs = lax.dynamic_slice(allowed, (l0, m0), (4, 2))
    inside = jnp.arange(B)[None, :] < block_units[:, None] * UNIT
    mask = (
        (pairs == 1)[:, :, None, None]
        & lax.dynamic_slice_in_dim(inside, l0, 4, 0)[:, None, :, None]
        & lax.dynamic_slice_in_dim(inside, m0, 2, 0)[None, :, None, :]
    )
    return jnp.where(mask, out, jnp.bfloat16(0))


def solution(mesh):
    fine = Mesh(mesh.devices.reshape(4, 2, 4, 4), ("x", "core", "y", "z"))
    return jax.shard_map(
        shards,
        mesh=fine,
        in_specs=(
            P(("y", "z"), None, None, None),
            P(("x", "core"), ("y", "z"), None, None),
            P(("x", "core"), ("y", "z"), None, None),
            P(),
            P(),
        ),
        out_specs=P(("x", "core"), ("y", "z"), None, None),
        check_vma=False,
    )
```

```python
import functools

import jax
import jax.numpy as jnp
from jax import lax
from jax.experimental import pallas as pl
from jax.experimental.pallas import tpu as pltpu
from jax.sharding import Mesh
from jax.sharding import PartitionSpec as P

B = 128
UNIT = B // 8
CHUNK = 4


def shifted(size, step):
    return [(i, (i + step) % size) for i in range(size)]


def products_kernel(late, terms, allowed, units, *refs):
    half = terms // 2
    pieces = 5 if late else 3
    lefts, refs = refs[:pieces], refs[pieces:]
    rights, refs = refs[:pieces], refs[pieces:]
    wave, refs = (refs[:1], refs[1:]) if late else (refs[:8], refs[8:])
    if late:
        refs = refs[4:]
    outs, refs = refs[:4], refs[4:]
    if not late:
        wave_out, *refs = refs
    ls, rs, w, t, sums, lists, counts, seen, started, sems, out_sems = refs
    y, z, x, c = (lax.axis_index(name) for name in ("y", "z", "x", "core"))
    whole = []

    def fetch(src, dst, sem):
        copy = pltpu.make_async_copy(src, dst, sem)
        copy.start()
        return copy

    if late:
        new = 2 * lax.rem(z + 2, 4)
        whole.append(
            fetch(wave[0].at[:, pl.ds(6, 2)], w.at[:, pl.ds(6, 2)], sems.at[16])
        )
        whole.append(
            fetch(
                wave[0].at[pl.ds(new, 2), pl.ds(0, 6)],
                w.at[pl.ds(new, 2), pl.ds(0, 6)],
                sems.at[17],
            )
        )
    else:
        for at in range(8):
            chip = lax.rem(x + 4 - at % 4, 4)
            whole.append(fetch(wave[at], w.at[2 * chip + (c ^ (at // 4))], sems.at[16 + at]))
    order = (6, 7, 0, 1, 2, 3, 4, 5) if late else range(6)
    turns = [(side, slot) for slot in order for side in range(2)]
    if late:
        turns.sort(key=lambda turn: (turn[0] == 0 and turn[1] < 6))
    for side, slot in turns:
        store, parts = ((ls, lefts), (rs, rights))[side]
        sem = sems.at[8 * side + slot]
        i = slot % 2
        if slot < 6:
            fetch(parts[slot // 2].at[:, i], store.at[slot], sem)
        else:
            for part in range(2):
                fetch(parts[3 + part].at[:, i], store.at[slot, pl.ds(half * part, half)], sem)
    for at in range(16):
        seen[at] = 0

    def ready(side, store, slot):
        at = 8 * side + slot

        @pl.when(seen[at] == 0)
        def _():
            pltpu.make_async_copy(store.at[slot], store.at[slot], sems.at[at]).wait()
            seen[at] = 1

    def shift_of(slot):
        pair = slot // 2
        return jnp.where(pair == 0, 0, jnp.where(pair == 1, 3, pair - 1))

    def left_sector(slot):
        return 8 * lax.rem(y + shift_of(slot), 4) + 2 * z + lax.rem(slot, 2)

    def right_local(slot):
        return 2 * lax.rem(z + shift_of(slot), 4) + lax.rem(slot, 2)

    for at in range(8):
        counts[at] = 0

    def enlist(slot):
        cls = allowed[left_sector(slot), 0]
        n = counts[cls]
        lists[8 * cls + n] = slot
        counts[cls] = n + 1
        cls = (allowed[0, 8 * y + right_local(slot)] == allowed[0, 0]).astype(jnp.int32)
        n = counts[2 + cls]
        lists[16 + 8 * cls + n] = slot
        counts[2 + cls] = n + 1

    if late:
        pl.loop(6, 8)(enlist)
        for at in range(4):
            counts[4 + at] = counts[at]
    pl.loop(0, 6)(enlist)
    if not late:
        for at in range(4):
            counts[4 + at] = counts[at]

    for copy in whole:
        copy.wait()

    if not late:
        row = lax.broadcasted_iota(jnp.int32, (B, B), 0)
        col = lax.broadcasted_iota(jnp.int32, (B, B), 1)

        @pl.loop(0, 8)
        def _(q):
            columns = (col < units[8 * y + q] * UNIT).astype(jnp.float32)
            for l in range(8):
                rows = (row < units[left_sector(l)] * UNIT).astype(jnp.float32)
                w[q, l] = w[q, l] * (rows * columns).astype(jnp.bfloat16)

        passed = fetch(w, wave_out, sems.at[16])
    counts[8] = 0

    def out_copy(other, to, e, i, j):
        return [
            pltpu.make_async_copy(
                sums.at[other, to, e, i, j],
                out.at[to, i, j],
                out_sems.at[(((other * 4 + to) * 2 + e) * 2 + i) * 2 + j],
            )
            for out in outs
        ]

    def item(left_slots, right_slots):
        nl, nm = len(left_slots), len(right_slots)
        locals_ = [right_local(m) for m in right_slots]
        for l in left_slots:
            ready(0, ls, l)
        for m in right_slots:
            ready(1, rs, m)
        for a, l in enumerate(left_slots):
            blocks = [w[q, l] for q in locals_]
            wide = blocks[0] if nm == 1 else jnp.concatenate(blocks, axis=1)
            for k0 in range(0, terms, CHUNK):
                n = min(CHUNK, terms - k0)
                part = jnp.dot(
                    ls[l, k0 : k0 + n].reshape(n * B, B), wide, preferred_element_type=jnp.float32
                ).astype(jnp.bfloat16).reshape(n, B, nm * B)
                for k in range(n):
                    for b in range(nm):
                        t[b, a * B : (a + 1) * B, (k0 + k) * B : (k0 + k + 1) * B] = part[k][
                            :, b * B : (b + 1) * B
                        ]
        for b, m in enumerate(right_slots):
            right = rs[m]
            wide = jnp.concatenate([right[k] for k in range(terms)], axis=1)
            total = lax.dot_general(
                t[b, : nl * B], wide, (((1,), (1,)), ((), ())), preferred_element_type=jnp.float32
            ).astype(jnp.bfloat16)
            owner = locals_[b] // 2
            e, j = lax.rem(owner, 2) ^ lax.rem(z, 2), lax.rem(locals_[b], 2)
            other = (owner // 2) ^ c
            for a, l in enumerate(left_slots):
                to = lax.rem(y + shift_of(l) + 4 - x, 4)
                sums[other, to, e, lax.rem(l, 2), j] = total[a * B : (a + 1) * B]
            for l in left_slots:
                to = lax.rem(y + shift_of(l) + 4 - x, 4)
                for at, copy in enumerate(out_copy(other, to, e, lax.rem(l, 2), j)):
                    pl.when(2 * other + e == at)(copy.start)
                n = counts[8]
                started[n] = (((other * 4 + to) * 2 + e) * 2 + lax.rem(l, 2)) * 2 + j
                counts[8] = n + 1

    def rectangle(cls, l0, nl, m0, nm):
        lb, mb = 8 * cls + l0, 16 + 8 * cls + m0

        @pl.loop(0, nl // 2)
        def _(a):
            pair = [lists[lb + 2 * a], lists[lb + 2 * a + 1]]

            @pl.loop(0, nm // 2)
            def _(b):
                item(pair, [lists[mb + 2 * b], lists[mb + 2 * b + 1]])

            @pl.when(lax.rem(nm, 2) == 1)
            def _():
                item(pair, [lists[mb + nm - 1]])

        @pl.when(lax.rem(nl, 2) == 1)
        def _():
            one = [lists[lb + nl - 1]]

            @pl.loop(0, nm // 2)
            def _(b):
                item(one, [lists[mb + 2 * b], lists[mb + 2 * b + 1]])

            @pl.when(lax.rem(nm, 2) == 1)
            def _():
                item(one, [lists[mb + nm - 1]])

    @pl.loop(0, 4 if late else 2)
    def _(turn):
        cls = lax.rem(turn, 2)
        old = turn // 2
        new_l, all_l = counts[4 + cls], counts[cls]
        new_m, all_m = counts[6 + cls], counts[2 + cls]
        rectangle(
            cls,
            jnp.where(old == 1, new_l, 0),
            jnp.where(old == 1, all_l - new_l, new_l),
            0,
            jnp.where(old == 1, new_m, all_m),
        )

    for slot in order:
        ready(0, ls, slot)
        ready(1, rs, slot)

    @pl.loop(0, counts[8])
    def _(n):
        pltpu.make_async_copy(
            sums.at[0, 0, 0, 0, 0], outs[0].at[0, 0, 0], out_sems.at[started[n]]
        ).wait()

    if not late:
        passed.wait()


def products(allowed, units, lefts, rights, wave, before=()):
    terms = lefts[0].shape[0]
    smem = pl.BlockSpec(memory_space=pltpu.SMEM)
    hbm = pl.BlockSpec(memory_space=pl.ANY)
    out = jax.ShapeDtypeStruct((4, 2, 2, B, B), jnp.bfloat16)
    masked = jax.ShapeDtypeStruct((8, 8, B, B), jnp.bfloat16)
    late = bool(before)
    n_in = 2 + 2 * len(lefts) + len(wave)
    return pl.pallas_call(
        functools.partial(products_kernel, late, terms),
        out_shape=(out,) * 4 if late else (out,) * 4 + (masked,),
        in_specs=[smem] * 2 + [hbm] * (n_in - 2 + len(before)),
        out_specs=(hbm,) * (4 if late else 5),
        input_output_aliases={n_in + at: at for at in range(len(before))},
        scratch_shapes=[
            pltpu.VMEM((8, terms, B, B), jnp.bfloat16),
            pltpu.VMEM((8, terms, B, B), jnp.bfloat16),
            pltpu.VMEM((8, 8, B, B), jnp.bfloat16),
            pltpu.VMEM((2, 2 * B, terms * B), jnp.bfloat16),
            pltpu.VMEM((2, 4, 2, 2, 2, B, B), jnp.bfloat16),
            pltpu.SMEM((32,), jnp.int32),
            pltpu.SMEM((9,), jnp.int32),
            pltpu.SMEM((16,), jnp.int32),
            pltpu.SMEM((64,), jnp.int32),
            pltpu.SemaphoreType.DMA((26,)),
            pltpu.SemaphoreType.DMA((64,)),
        ],
        compiler_params=pltpu.CompilerParams(vmem_limit_bytes=58 * 2**20),
        cost_estimate=pl.CostEstimate(
            flops=32 * terms * 4 * B**3, bytes_accessed=14 * 2**20, transcendentals=0
        ),
    )(allowed, units, *lefts, *rights, *wave, *before)


def ring_near(own, axis):
    return lax.ppermute(own, axis, shifted(4, 1)), lax.ppermute(own, axis, shifted(4, -1))


def far_half(near):
    half = near[0].shape[0] // 2
    return near[0][:half], near[1][half:]


def ring_far(halves, axis):
    return (
        lax.ppermute(halves[0], axis, shifted(4, 1)),
        lax.ppermute(halves[1], axis, shifted(4, -1)),
    )


def swapped(size, bit):
    return [(i, i ^ bit) for i in range(size)]


def gather_wave(wavefunction, y, q, operators):
    def toward(owner):
        return lax.dynamic_slice_in_dim(wavefunction, 8 * owner + q, 1, 1)[:, 0]

    moved = [lax.ppermute(toward((y + d) % 4), "y", shifted(4, d)) for d in (1, 3, 2)]
    left, right = operators
    first, right = lax.optimization_barrier((moved[0], right))
    moved, left = lax.optimization_barrier(([first] + moved[1:], left))
    operators = left, right
    mine = jnp.concatenate([toward(y)] + moved)
    row = [mine] + [lax.ppermute(mine, "x", shifted(4, d)) for d in (1, 2, 3)]
    return row, operators


def share_wave(row):
    return (*row, *(lax.ppermute(part, "core", swapped(2, 1)) for part in row))


def add_cores(keep, send):
    other = lax.ppermute(send, "core", shifted(2, 1))
    both = [keep[d].astype(jnp.float32) + other[d].astype(jnp.float32) for d in range(4)]
    return both[0], [part.astype(jnp.bfloat16) for part in both[1:]]


def add_send(chips):
    return [lax.ppermute(part, "x", shifted(4, d + 1)) for d, part in enumerate(chips)]


def add_chips(own, chips):
    return (own + sum(part.astype(jnp.float32) for part in chips)).astype(jnp.bfloat16)


def shards(wavefunction, left_operator, right_operator, allowed, block_units):
    x, c = lax.axis_index("x"), lax.axis_index("core")
    y, z = lax.axis_index("y"), lax.axis_index("z")
    q = 2 * x + c
    row, (left_operator, right_operator) = gather_wave(
        wavefunction, y, q, (left_operator, right_operator)
    )
    near_l, near_r = ring_near(left_operator, "y"), ring_near(right_operator, "z")
    row, *near_l = lax.optimization_barrier((row, *near_l))
    wave = share_wave(row)
    lefts, rights = (left_operator, *near_l), (right_operator, *near_r)
    far_l, far_r = far_half(near_l), far_half(near_r)
    *sums, masked = products(allowed, block_units, lefts, rights, wave)
    lefts = (*lefts, *ring_far(far_l, "y"))
    rights = (*rights, *ring_far(far_r, "z"))
    sums = products(allowed, block_units, lefts, rights, (masked,), sums)
    halves = [add_cores(sums[s], sums[2 + s]) for s in range(2)]
    halves = [(own, add_send(chips)) for own, chips in halves]

    got = []
    for s in range(2):
        perm = [
            (cc * 4 + zz, (zz // 2) * 4 + 2 * cc + (s ^ (zz & 1)))
            for cc in range(2)
            for zz in range(4)
        ]
        half, got = lax.optimization_barrier((halves[s], got))
        got.append(lax.ppermute(add_chips(*half), ("core", "z"), perm))
    odd = (z & 1) == 1
    first = jnp.where(odd, got[1], got[0])
    second = jnp.where(odd, got[0], got[1])
    out = jnp.concatenate([first, second], axis=0)
    l0, m0 = 8 * x + 4 * c, 8 * y + 2 * z
    pairs = lax.dynamic_slice(allowed, (l0, m0), (4, 2))
    inside = jnp.arange(B)[None, :] < block_units[:, None] * UNIT
    mask = (
        (pairs == 1)[:, :, None, None]
        & lax.dynamic_slice_in_dim(inside, l0, 4, 0)[:, None, :, None]
        & lax.dynamic_slice_in_dim(inside, m0, 2, 0)[None, :, None, :]
    )
    return jnp.where(mask, out, jnp.bfloat16(0))


def solution(mesh):
    fine = Mesh(mesh.devices.reshape(4, 2, 4, 4), ("x", "core", "y", "z"))
    return jax.shard_map(
        shards,
        mesh=fine,
        in_specs=(
            P(("y", "z"), None, None, None),
            P(("x", "core"), ("y", "z"), None, None),
            P(("x", "core"), ("y", "z"), None, None),
            P(),
            P(),
        ),
        out_specs=P(("x", "core"), ("y", "z"), None, None),
        check_vma=False,
    )
```

```python
import functools

import jax
import jax.numpy as jnp
from jax import lax
from jax.experimental import pallas as pl
from jax.experimental.pallas import tpu as pltpu
from jax.sharding import Mesh
from jax.sharding import PartitionSpec as P

B = 128
UNIT = B // 8
CHUNK = 4


def shifted(size, step):
    return [(i, (i + step) % size) for i in range(size)]


def products_kernel(late, terms, allowed, units, *refs):
    half = terms // 2
    pieces = 5 if late else 3
    lefts, refs = refs[:pieces], refs[pieces:]
    rights, refs = refs[:pieces], refs[pieces:]
    wave, refs = (refs[:1], refs[1:]) if late else (refs[:8], refs[8:])
    if late:
        refs = refs[4:]
    outs, refs = refs[:4], refs[4:]
    if not late:
        wave_out, *refs = refs
    ls, rs, w, t, sums, lists, counts, seen, started, sems, out_sems = refs
    y, z, x, c = (lax.axis_index(name) for name in ("y", "z", "x", "core"))
    whole = []

    def fetch(src, dst, sem):
        copy = pltpu.make_async_copy(src, dst, sem)
        copy.start()
        return copy

    if late:
        new = 2 * lax.rem(z + 2, 4)
        whole.append(
            fetch(wave[0].at[:, pl.ds(6, 2)], w.at[:, pl.ds(6, 2)], sems.at[16])
        )
        whole.append(
            fetch(
                wave[0].at[pl.ds(new, 2), pl.ds(0, 6)],
                w.at[pl.ds(new, 2), pl.ds(0, 6)],
                sems.at[17],
            )
        )
    else:
        for at in range(8):
            chip = lax.rem(x + 4 - at % 4, 4)
            whole.append(fetch(wave[at], w.at[2 * chip + (c ^ (at // 4))], sems.at[16 + at]))
    order = (6, 7, 0, 1, 2, 3, 4, 5) if late else range(6)
    turns = [(side, slot) for slot in order for side in range(2)]
    if late:
        turns.sort(key=lambda turn: (turn[0] == 0 and turn[1] < 6))
    for side, slot in turns:
        store, parts = ((ls, lefts), (rs, rights))[side]
        sem = sems.at[8 * side + slot]
        i = slot % 2
        if slot < 6:
            fetch(parts[slot // 2].at[:, i], store.at[slot], sem)
        else:
            for part in range(2):
                fetch(parts[3 + part].at[:, i], store.at[slot, pl.ds(half * part, half)], sem)
    for at in range(16):
        seen[at] = 0

    def ready(side, store, slot):
        at = 8 * side + slot

        @pl.when(seen[at] == 0)
        def _():
            pltpu.make_async_copy(store.at[slot], store.at[slot], sems.at[at]).wait()
            seen[at] = 1

    def shift_of(slot):
        pair = slot // 2
        return jnp.where(pair == 0, 0, jnp.where(pair == 1, 3, pair - 1))

    def left_sector(slot):
        return 8 * lax.rem(y + shift_of(slot), 4) + 2 * z + lax.rem(slot, 2)

    def right_local(slot):
        return 2 * lax.rem(z + shift_of(slot), 4) + lax.rem(slot, 2)

    for at in range(8):
        counts[at] = 0

    def enlist(slot):
        cls = allowed[left_sector(slot), 0]
        n = counts[cls]
        lists[8 * cls + n] = slot
        counts[cls] = n + 1
        cls = (allowed[0, 8 * y + right_local(slot)] == allowed[0, 0]).astype(jnp.int32)
        n = counts[2 + cls]
        lists[16 + 8 * cls + n] = slot
        counts[2 + cls] = n + 1

    if late:
        pl.loop(6, 8)(enlist)
        for at in range(4):
            counts[4 + at] = counts[at]
    pl.loop(0, 6)(enlist)
    if not late:
        for at in range(4):
            counts[4 + at] = counts[at]

    for copy in whole:
        copy.wait()

    if not late:
        row = lax.broadcasted_iota(jnp.int32, (B, B), 0)
        col = lax.broadcasted_iota(jnp.int32, (B, B), 1)

        @pl.loop(0, 8)
        def _(q):
            columns = (col < units[8 * y + q] * UNIT).astype(jnp.float32)
            for l in range(8):
                rows = (row < units[left_sector(l)] * UNIT).astype(jnp.float32)
                w[q, l] = w[q, l] * (rows * columns).astype(jnp.bfloat16)

        passed = fetch(w, wave_out, sems.at[16])
    counts[8] = 0

    def out_copy(other, to, e, i, j):
        return [
            pltpu.make_async_copy(
                sums.at[other, to, e, i, j],
                out.at[to, i, j],
                out_sems.at[(((other * 4 + to) * 2 + e) * 2 + i) * 2 + j],
            )
            for out in outs
        ]

    def item(left_slots, right_slots):
        nl, nm = len(left_slots), len(right_slots)
        locals_ = [right_local(m) for m in right_slots]
        for l in left_slots:
            ready(0, ls, l)
        for m in right_slots:
            ready(1, rs, m)
        for a, l in enumerate(left_slots):
            blocks = [w[q, l] for q in locals_]
            wide = blocks[0] if nm == 1 else jnp.concatenate(blocks, axis=1)
            for k0 in range(0, terms, CHUNK):
                n = min(CHUNK, terms - k0)
                part = jnp.dot(
                    ls[l, k0 : k0 + n].reshape(n * B, B), wide, preferred_element_type=jnp.float32
                ).astype(jnp.bfloat16).reshape(n, B, nm * B)
                for k in range(n):
                    for b in range(nm):
                        t[b, a * B : (a + 1) * B, (k0 + k) * B : (k0 + k + 1) * B] = part[k][
                            :, b * B : (b + 1) * B
                        ]
        for b, m in enumerate(right_slots):
            right = rs[m]
            wide = jnp.concatenate([right[k] for k in range(terms)], axis=1)
            total = lax.dot_general(
                t[b, : nl * B], wide, (((1,), (1,)), ((), ())), preferred_element_type=jnp.float32
            ).astype(jnp.bfloat16)
            owner = locals_[b] // 2
            e, j = lax.rem(owner, 2) ^ lax.rem(z, 2), lax.rem(locals_[b], 2)
            other = (owner // 2) ^ c
            for a, l in enumerate(left_slots):
                to = lax.rem(y + shift_of(l) + 4 - x, 4)
                sums[other, to, e, lax.rem(l, 2), j] = total[a * B : (a + 1) * B]
            for l in left_slots:
                to = lax.rem(y + shift_of(l) + 4 - x, 4)
                for at, copy in enumerate(out_copy(other, to, e, lax.rem(l, 2), j)):
                    pl.when(2 * other + e == at)(copy.start)
                n = counts[8]
                started[n] = (((other * 4 + to) * 2 + e) * 2 + lax.rem(l, 2)) * 2 + j
                counts[8] = n + 1

    def rectangle(cls, l0, nl, m0, nm):
        lb, mb = 8 * cls + l0, 16 + 8 * cls + m0

        @pl.loop(0, nl // 2)
        def _(a):
            pair = [lists[lb + 2 * a], lists[lb + 2 * a + 1]]

            @pl.loop(0, nm // 2)
            def _(b):
                item(pair, [lists[mb + 2 * b], lists[mb + 2 * b + 1]])

            @pl.when(lax.rem(nm, 2) == 1)
            def _():
                item(pair, [lists[mb + nm - 1]])

        @pl.when(lax.rem(nl, 2) == 1)
        def _():
            one = [lists[lb + nl - 1]]

            @pl.loop(0, nm // 2)
            def _(b):
                item(one, [lists[mb + 2 * b], lists[mb + 2 * b + 1]])

            @pl.when(lax.rem(nm, 2) == 1)
            def _():
                item(one, [lists[mb + nm - 1]])

    @pl.loop(0, 4 if late else 2)
    def _(turn):
        cls = lax.rem(turn, 2)
        old = turn // 2
        new_l, all_l = counts[4 + cls], counts[cls]
        new_m, all_m = counts[6 + cls], counts[2 + cls]
        rectangle(
            cls,
            jnp.where(old == 1, new_l, 0),
            jnp.where(old == 1, all_l - new_l, new_l),
            0,
            jnp.where(old == 1, new_m, all_m),
        )

    for slot in order:
        ready(0, ls, slot)
        ready(1, rs, slot)

    @pl.loop(0, counts[8])
    def _(n):
        pltpu.make_async_copy(
            sums.at[0, 0, 0, 0, 0], outs[0].at[0, 0, 0], out_sems.at[started[n]]
        ).wait()

    if not late:
        passed.wait()


def products(allowed, units, lefts, rights, wave, before=()):
    terms = lefts[0].shape[0]
    smem = pl.BlockSpec(memory_space=pltpu.SMEM)
    hbm = pl.BlockSpec(memory_space=pl.ANY)
    out = jax.ShapeDtypeStruct((4, 2, 2, B, B), jnp.bfloat16)
    masked = jax.ShapeDtypeStruct((8, 8, B, B), jnp.bfloat16)
    late = bool(before)
    n_in = 2 + 2 * len(lefts) + len(wave)
    return pl.pallas_call(
        functools.partial(products_kernel, late, terms),
        out_shape=(out,) * 4 if late else (out,) * 4 + (masked,),
        in_specs=[smem] * 2 + [hbm] * (n_in - 2 + len(before)),
        out_specs=(hbm,) * (4 if late else 5),
        input_output_aliases={n_in + at: at for at in range(len(before))},
        scratch_shapes=[
            pltpu.VMEM((8, terms, B, B), jnp.bfloat16),
            pltpu.VMEM((8, terms, B, B), jnp.bfloat16),
            pltpu.VMEM((8, 8, B, B), jnp.bfloat16),
            pltpu.VMEM((2, 2 * B, terms * B), jnp.bfloat16),
            pltpu.VMEM((2, 4, 2, 2, 2, B, B), jnp.bfloat16),
            pltpu.SMEM((32,), jnp.int32),
            pltpu.SMEM((9,), jnp.int32),
            pltpu.SMEM((16,), jnp.int32),
            pltpu.SMEM((64,), jnp.int32),
            pltpu.SemaphoreType.DMA((26,)),
            pltpu.SemaphoreType.DMA((64,)),
        ],
        compiler_params=pltpu.CompilerParams(vmem_limit_bytes=59 * 2**20),
        cost_estimate=pl.CostEstimate(
            flops=32 * terms * 4 * B**3, bytes_accessed=14 * 2**20, transcendentals=0
        ),
    )(allowed, units, *lefts, *rights, *wave, *before)


def ring_near(own, axis):
    return lax.ppermute(own, axis, shifted(4, 1)), lax.ppermute(own, axis, shifted(4, -1))


def far_half(near):
    half = near[0].shape[0] // 2
    return near[0][:half], near[1][half:]


def ring_far(halves, axis):
    return (
        lax.ppermute(halves[0], axis, shifted(4, 1)),
        lax.ppermute(halves[1], axis, shifted(4, -1)),
    )


def swapped(size, bit):
    return [(i, i ^ bit) for i in range(size)]


def gather_wave(wavefunction, y, q, operators):
    def toward(owner):
        return lax.dynamic_slice_in_dim(wavefunction, 8 * owner + q, 1, 1)[:, 0]

    moved = [lax.ppermute(toward((y + d) % 4), "y", shifted(4, d)) for d in (1, 3, 2)]
    left, right = operators
    first, right = lax.optimization_barrier((moved[0], right))
    moved, left = lax.optimization_barrier(([first] + moved[1:], left))
    operators = left, right
    mine = jnp.concatenate([toward(y)] + moved)
    row = [mine] + [lax.ppermute(mine, "x", shifted(4, d)) for d in (1, 2, 3)]
    return row, operators


def share_wave(row):
    return (*row, *(lax.ppermute(part, "core", swapped(2, 1)) for part in row))


def add_cores(keep, send):
    other = lax.ppermute(send, "core", shifted(2, 1))
    both = [keep[d].astype(jnp.float32) + other[d].astype(jnp.float32) for d in range(4)]
    return both[0], [part.astype(jnp.bfloat16) for part in both[1:]]


def add_send(chips):
    return [lax.ppermute(part, "x", shifted(4, d + 1)) for d, part in enumerate(chips)]


def add_chips(own, chips):
    return (own + sum(part.astype(jnp.float32) for part in chips)).astype(jnp.bfloat16)


def shards(wavefunction, left_operator, right_operator, allowed, block_units):
    x, c = lax.axis_index("x"), lax.axis_index("core")
    y, z = lax.axis_index("y"), lax.axis_index("z")
    q = 2 * x + c
    row, (left_operator, right_operator) = gather_wave(
        wavefunction, y, q, (left_operator, right_operator)
    )
    near_l, near_r = ring_near(left_operator, "y"), ring_near(right_operator, "z")
    row, *near_l = lax.optimization_barrier((row, *near_l))
    wave = share_wave(row)
    lefts, rights = (left_operator, *near_l), (right_operator, *near_r)
    far_l, far_r = far_half(near_l), far_half(near_r)
    *sums, masked = products(allowed, block_units, lefts, rights, wave)
    lefts = (*lefts, *ring_far(far_l, "y"))
    rights = (*rights, *ring_far(far_r, "z"))
    sums = products(allowed, block_units, lefts, rights, (masked,), sums)
    halves = [add_cores(sums[s], sums[2 + s]) for s in range(2)]
    halves = [(own, add_send(chips)) for own, chips in halves]

    got = []
    for s in range(2):
        perm = [
            (cc * 4 + zz, (zz // 2) * 4 + 2 * cc + (s ^ (zz & 1)))
            for cc in range(2)
            for zz in range(4)
        ]
        half, got = lax.optimization_barrier((halves[s], got))
        got.append(lax.ppermute(add_chips(*half), ("core", "z"), perm))
    odd = (z & 1) == 1
    first = jnp.where(odd, got[1], got[0])
    second = jnp.where(odd, got[0], got[1])
    out = jnp.concatenate([first, second], axis=0)
    l0, m0 = 8 * x + 4 * c, 8 * y + 2 * z
    pairs = lax.dynamic_slice(allowed, (l0, m0), (4, 2))
    inside = jnp.arange(B)[None, :] < block_units[:, None] * UNIT
    mask = (
        (pairs == 1)[:, :, None, None]
        & lax.dynamic_slice_in_dim(inside, l0, 4, 0)[:, None, :, None]
        & lax.dynamic_slice_in_dim(inside, m0, 2, 0)[None, :, None, :]
    )
    return jnp.where(mask, out, jnp.bfloat16(0))


def solution(mesh):
    fine = Mesh(mesh.devices.reshape(4, 2, 4, 4), ("x", "core", "y", "z"))
    return jax.shard_map(
        shards,
        mesh=fine,
        in_specs=(
            P(("y", "z"), None, None, None),
            P(("x", "core"), ("y", "z"), None, None),
            P(("x", "core"), ("y", "z"), None, None),
            P(),
            P(),
        ),
        out_specs=P(("x", "core"), ("y", "z"), None, None),
        check_vma=False,
    )
```
